32 devices in a mesh: section: 4 (over y, x), elem: 8 (over z, core).
Axes of the slice: x: 2, y: 2, z: 4, core: 2. Of those that a mesh axis runs over, the one named last changes fastest.
Arguments:
- interior_res: bfloat16 [3, 8, 4, 48, 100], P(None, 'elem', 'section'), may hold values from -1.5 to 1.5
- face_res: bfloat16 [3, 8, 4, 48, 4, 50], P(None, 'elem', 'section'), may hold values from -1.5 to 1.5
- trace_vals: bfloat16 [3, 8, 4, 48, 4, 50], P(None, 'elem', 'section'), may hold values from -1.5 to 1.5
- stabil: bfloat16 [8, 4, 48, 4, 25], P('elem'), may hold values from -2.5 to 2.5
- element_faces: int32 [8, 4, 48, 4], P('elem'), may hold values from 0 to 3071, as said below
- orient: int32 [8, 4, 48, 4, 10], P('elem'), may hold values from 0 to 9, as said below
- lift_matrix: bfloat16 [4, 20, 10], replicated, may hold values from -2 to 2
- face_matrix: bfloat16 [10, 10], replicated, may hold values from -2 to 2
- factors: bfloat16 [4, 8, 100, 19200], P('section', 'elem'), may hold values from -0.625 to 0.625
Outputs:
- trace_residual: float32 [3, 3072, 50], P(None, ('section', 'elem'))
- schur_product: float32 [3, 3072, 50], P(None, ('section', 'elem'))
The draws below stay inside these ranges and needn't reach their ends.
Inputs may be any that keep to these rules, and one draw needn't show every extreme that they name: `element_faces`: every face number is named by exactly two element faces. Face f is owned by column (f // 96) % 8. For every other column, exactly 2 of a column's element faces name faces owned by that column; the rest name faces owned by the column itself. `orient`: each row of 10 numbers is one of the six node orders that the symmetries of a triangle give to the ten nodes of its degree-3 lattice.
All inputs are finite; a program needn't handle non-finite values.
Results may differ from the reference program's by a relative error of at most 0.004.
Values may be sent and summed in bfloat16 or wider, within the bound.
A program may use at most 128 MiB of HBM per device.

```python
import jax
import jax.numpy as jnp
import numpy as np
from jax import lax

VARS = 5
MODES = 20
FNODES = 10
ELEMS = 48
NI = 100
NF = 50
COLS = 8
COL_ELEMS = 192
GROUP_ELEMS = 64
SHARE = 2
FACE_DEV = 96
FACES = 3072
N_SECTION = 4


def triangle_table():
    lattice = [(first, second, 3 - first - second) for first in range(4) for second in range(4 - first)]
    rotations = [(0, 1, 2), (1, 2, 0), (2, 0, 1), (0, 2, 1), (2, 1, 0), (1, 0, 2)]
    table_rows = []
    for rotation in rotations:
        table_rows.append([lattice.index(tuple((point[corner] for corner in rotation))) for point in lattice])
    return np.array(table_rows, dtype=np.int32)


def draw_orient(key, part):
    symmetry = jax.random.randint(jax.random.fold_in(key, 5), (COLS, 4, ELEMS, 4), 0, 6)
    return jnp.asarray(triangle_table())[symmetry].astype(jnp.int32)


def draw_element_faces(key, part):
    item_count = 16 * ELEMS
    owned_count = 8 * ELEMS
    pair_faces = 2 * SHARE
    boundary_count = (COLS - 1) * pair_faces
    column_keys = jax.random.split(jax.random.fold_in(key, 11), COLS)
    owner_keys = jax.random.split(jax.random.fold_in(key, 12), COLS)
    orders = jax.vmap(lambda subkey: jax.random.permutation(subkey, item_count))(column_keys)
    places = jnp.argsort(orders, axis=1).astype(jnp.int32)
    columns = jnp.arange(COLS, dtype=jnp.int32)[:, None]
    boundary = places < boundary_count
    distance = places // pair_faces + 1
    within = places % pair_faces
    other_col = (columns + distance) % COLS
    self_owns = within < SHARE
    boundary_owner = jnp.where(self_owns, columns, other_col)
    boundary_number = jnp.where(self_owns, (distance - 1) * SHARE + within, (COLS - distance - 1) * SHARE + (within - SHARE))
    inner_number = (COLS - 1) * SHARE + (places - boundary_count) // 2
    owner = jnp.where(boundary, boundary_owner, columns)
    number = jnp.where(boundary, boundary_number, inner_number)
    owner_orders = jax.vmap(lambda subkey: jax.random.permutation(subkey, owned_count))(owner_keys)
    slot_place = owner_orders[owner, number]
    block = slot_place // FACE_DEV
    within_block = slot_place % FACE_DEV
    face = (block * COLS + owner) * FACE_DEV + within_block
    return face.reshape(COLS, 4, ELEMS, 4).astype(jnp.int32)


def level_of(own_key, extent, shards, least, high):
    gain, own = 1.0, jax.random.fold_in(own_key, 6)
    for position, shards_of in shards:
        heights = jnp.exp(jax.random.uniform(jax.random.fold_in(own, position), (shards_of,), jnp.float32, least / len(shards), high / len(shards)))
        gain = gain * jnp.repeat(heights, extent[position] // shards_of).reshape([-1 if axis == position else 1 for axis in range(len(extent))])
    return gain


def bell_draw(own_key, extent, deviation, bound, pieces=(), kind=jnp.bfloat16):
    drawn = deviation * jax.random.normal(own_key, extent, jnp.float32)
    if pieces:
        drawn = drawn * level_of(own_key, extent, pieces, -0.22, 0.18)
    return jnp.clip(drawn, -bound, bound).astype(kind)


def setup_inputs(seed: int = 0) -> dict:
    keys = jax.random.split(jax.random.key(seed), 10)
    interior_res = bell_draw(keys[0], (3, COLS, N_SECTION, ELEMS, NI), 0.25, 1.5, ((1, 8), (2, 4)))
    face_res = bell_draw(keys[1], (3, COLS, N_SECTION, ELEMS, 4, NF), 0.25, 1.5, ((1, 8), (2, 4)))
    trace_vals = bell_draw(keys[2], (3, COLS, N_SECTION, ELEMS, 4, NF), 0.25, 1.5, ((1, 8), (2, 4)))
    stabil = bell_draw(keys[3], (COLS, N_SECTION, ELEMS, 4, VARS * VARS), VARS ** -0.5, 2.5, ((0, 8),))
    element_faces = draw_element_faces(jax.random.fold_in(keys[9], 71), 0)
    orient = draw_orient(jax.random.fold_in(keys[9], 71), 0)
    lift_matrix = bell_draw(keys[6], (4, MODES, FNODES), FNODES ** -0.5, 2.0)
    face_matrix = bell_draw(keys[7], (FNODES, FNODES), FNODES ** -0.5, 2.0)
    factors = bell_draw(keys[8], (N_SECTION, COLS, NI, COL_ELEMS * NI), NI ** -0.5, 0.625, ((0, 4), (1, 8)))
    return {"interior_res": interior_res, "face_res": face_res, "trace_vals": trace_vals, "stabil": stabil, "element_faces": element_faces, "orient": orient, "lift_matrix": lift_matrix, "face_matrix": face_matrix, "factors": factors}


radau_inverse = ((4.3255798900631553510, 0.33919925181580986954, 0.54177053993587487119),
                 (-4.1787185915519047273, -0.32768282076106238708, 0.47662355450055045196),
                 (-0.50287263494578687595, 2.5719269498556054292, -0.59603920482822492497))


def transform(sections):
    values = sections.astype(jnp.float32)
    return jnp.stack([radau_inverse[row_index][0] * values[0] + radau_inverse[row_index][1] * values[1]
                      + radau_inverse[row_index][2] * values[2] for row_index in range(3)]).astype(jnp.bfloat16)


def reference(interior_res, face_res, trace_vals, stabil, element_faces, orient, lift_matrix, face_matrix, factors):
    highest = lax.Precision.HIGHEST
    lift_wide = lift_matrix.astype(jnp.float32)
    mass_wide = face_matrix.astype(jnp.float32)
    inner_all = jnp.moveaxis(transform(interior_res), 1, 0)
    face_all = jnp.moveaxis(transform(face_res), 1, 0)
    trace_all = jnp.moveaxis(transform(trace_vals), 1, 0)
    factor_all = jnp.moveaxis(factors, 1, 0)

    def alternate(block):
        return block.reshape(3, NI, 4, ELEMS // 3, NI).transpose(1, 2, 3, 0, 4).reshape(NI, COL_ELEMS, NI)

    def column_terms(packed_col):
        inner_w, face_w, trace_w, stabil_col, factor_col = packed_col
        inner_part = inner_w.reshape(3, COL_ELEMS, NI)
        face_part = face_w.reshape(3, COL_ELEMS, 4, FNODES, VARS).astype(jnp.float32)
        trace_part = trace_w.reshape(3, COL_ELEMS, 4, FNODES, VARS).astype(jnp.float32)
        stab_wide = stabil_col.reshape(COL_ELEMS, 4, VARS, VARS).astype(jnp.float32)
        weighted = jnp.einsum('ekvu,ceknu->ceknv', stab_wide, trace_part, precision=highest)
        lifted = jnp.einsum('kmn,ceknv->cemv', lift_wide, weighted, precision=highest)
        lifted = lifted.reshape(3, COL_ELEMS, NI).astype(jnp.bfloat16)
        right_sides = jnp.stack([inner_part, lifted], 1).astype(jnp.float32)
        real_inverse = factor_col[0].astype(jnp.float32).reshape(NI, COL_ELEMS, NI)
        first = jnp.einsum('iej,rej->rei', real_inverse, right_sides[0], precision=highest)
        real_part = alternate(factor_col[1:, :, :GROUP_ELEMS * NI].astype(jnp.float32))
        imag_part = alternate(factor_col[1:, :, GROUP_ELEMS * NI:2 * GROUP_ELEMS * NI].astype(jnp.float32))
        by_real = jnp.einsum('iej,crej->crei', real_part, right_sides[1:], precision=highest)
        by_imag = jnp.einsum('iej,crej->crei', imag_part, right_sides[1:], precision=highest)
        solved = jnp.stack([first, by_real[0] - by_imag[1], by_imag[0] + by_real[1]])
        shaped = solved.reshape(3, 2, COL_ELEMS, MODES, VARS)
        weighted_solve = jnp.einsum('ekvu,cremu->crekmv', stab_wide, shaped, precision=highest)
        coupled = jnp.einsum('kmn,crekmv->creknv', lift_wide, weighted_solve, precision=highest)
        face_term = jnp.einsum('nj,cekjv->ceknv', mass_wide, weighted, precision=highest)
        return jnp.stack([face_part - coupled[:, 0], face_term - coupled[:, 1]], 1)

    contribs = lax.map(column_terms, (inner_all, face_all, trace_all, stabil, factor_all))
    node_order = orient.reshape(COLS, 1, 1, COL_ELEMS, 4, FNODES, 1).astype(jnp.int32)
    oriented = jnp.take_along_axis(contribs, node_order, axis=5)
    item_rows = oriented.transpose(0, 3, 4, 1, 2, 5, 6).reshape(COLS * COL_ELEMS * 4, 6 * NF)
    summed = jax.ops.segment_sum(item_rows, element_faces.reshape(-1), num_segments=FACES)
    summed = summed.reshape(FACES, 3, 2, NF)
    return summed[:, :, 0].transpose(1, 0, 2), summed[:, :, 1].transpose(1, 0, 2)
```

```python
import functools

import jax
import jax.numpy as jnp
import numpy as np
from jax import lax
from jax.experimental import pallas as pl
from jax.experimental.pallas import tpu as pltpu
from jax.sharding import PartitionSpec as P

radau_inverse = (
    (4.325579890063155, 0.33919925181580984, 0.5417705399358749),
    (-4.178718591551905, -0.32768282076106237, 0.47662355450055044),
    (-0.5028726349457868, 2.571926949855605, -0.5960392048282249),
)
LANE = 128
HALF = 64
MESH = pl.DeviceIdType.MESH


def triangle_table(fnodes):
    degree = next(d for d in range(1, fnodes) if (d + 1) * (d + 2) // 2 == fnodes)
    lattice = [(a, b, degree - a - b) for a in range(degree + 1) for b in range(degree + 1 - a)]
    rotations = [(0, 1, 2), (1, 2, 0), (2, 0, 1), (0, 2, 1), (2, 1, 0), (1, 0, 2)]
    return [
        [lattice.index(tuple(point[corner] for corner in rotation)) for point in lattice]
        for rotation in rotations
    ]


def structure(modes, fnodes, nvar, elems, chunk):
    lane = np.arange(LANE)
    side, inside = lane // HALF, lane % HALF
    node, var = inside // nvar, inside % nvar
    used = inside < fnodes * nvar
    inner = modes * nvar
    parts, place, at = [], {}, 0

    def add(name, block):
        nonlocal at
        rows, cols = block.shape
        wide = -(-cols // LANE) * LANE
        full = np.zeros((LANE, wide), np.float32)
        full[:rows, :cols] = block
        place[name] = (at, at + wide)
        parts.append(full)
        at += wide

    row = lane[:, None]
    expand, shifts, top, bottom = [], [], [], []
    for d in range(nvar):
        other = (var + d) % nvar
        expand.append((row == (var * nvar + other)[None]) & used[None])
        shifts.append(
            (row == (side * HALF + node * nvar + other)[None]) & (used & (side == 1))[None]
        )
        fit = (row % nvar == other[None]) & used[None] & (row < inner)
        top.append(fit & (side == 0)[None])
        bottom.append(fit & (side == 1)[None])
    expand.append((row == nvar * nvar) & np.ones((1, LANE), bool))
    add("expand", np.concatenate(expand, 1))
    add("shifts", np.concatenate(shifts, 1))
    add("top", np.concatenate(top, 1))
    add("bottom", np.concatenate(bottom, 1))
    add("modes", (row // nvar == np.arange(modes)[None]) & (row < inner))
    nodes = (np.arange(fnodes)[:, None] == node[None]) & used[None]
    add("nodes", np.concatenate([nodes] * nvar, 1))
    add("rows_node", nodes.T)
    one = used & (side == 1)
    add("same", (var[:, None] == var[None]) & one[:, None] & one[None])
    table = triangle_table(fnodes)
    turns = []
    for order in table:
        order = np.array(order + [0] * HALF)
        source = side * HALF + order[node] * nvar + var
        turns.append((row == source[None]) & used[None])
    add("turns", np.concatenate(turns, 1))
    column = np.arange(chunk * inner)
    add("repeat", row == (column % inner)[None])
    third = elems // 3
    r = np.arange(elems)
    add("thirds", (3 * (r % third) + r // third)[:, None] == r[None])
    return np.concatenate(parts, 1), place, [order[1] for order in table]


def dot(a, b):
    return jnp.dot(a, b, preferred_element_type=jnp.float32)


def dot_nt(a, b):
    return lax.dot_general(a, b, (((1,), (1,)), ((), ())), preferred_element_type=jnp.float32)


def split(x):
    high = x.astype(jnp.bfloat16)
    low = (x - high.astype(jnp.float32)).astype(jnp.bfloat16)
    return jnp.concatenate([high, low], axis=0)


def kernel(
    dims,
    place,
    classes,
    pack_ref,
    meta_ref,
    ids_ref,
    lift_ref,
    face_ref,
    const_ref,
    factor_hbm,
    out_res,
    out_schur,
    factor,
    send1,
    recv1,
    weights,
    stab,
    base,
    solved,
    send2,
    recv2,
    sums,
    send3,
    recv3,
    factor_sem,
    s1,
    r1,
    s2,
    r2,
    s3,
    r3,
):
    sections, columns, elems, inner, face_size, nvar, chunk = dims
    third = elems // 3
    col_elems = sections * elems
    face_dev = 2 * elems
    col_faces = sections * face_dev
    width = nvar * LANE
    f32, bf16 = jnp.float32, jnp.bfloat16
    section = lax.axis_index("section")
    column = lax.axis_index("elem")

    def const(name):
        lo, hi = place[name]
        return const_ref[:, lo:hi]

    factor_copy = pltpu.make_async_copy(factor_hbm.at[0, 0], factor, factor_sem)
    factor_copy.start()
    barrier = pltpu.get_barrier_semaphore()
    for d in range(1, sections):
        pl.semaphore_signal(
            barrier, inc=1, device_id={"section": lax.rem(section + d, sections)}, device_id_type=MESH
        )

    def greet(d, carry):
        pl.semaphore_signal(
            barrier, inc=1, device_id={"elem": lax.rem(column + d, columns)}, device_id_type=MESH
        )
        return carry

    lax.fori_loop(1, columns, greet, 0)

    send1[...] = jnp.zeros(send1.shape, bf16)
    thirds = const("thirds")[:elems, :elems]
    for part in range(5):
        values = [pack_ref[t, part].astype(f32) for t in range(3)]
        for g in range(3):
            row = radau_inverse[g]
            w = (row[0] * values[0] + row[1] * values[1] + row[2] * values[2]).astype(bf16)
            if g == 0:
                send1[0, part] = w
            else:
                w = dot(thirds, w).astype(bf16)
                for t in range(3):
                    send1[1 + t, part, (g - 1) * third : g * third] = w[t * third : (t + 1) * third]

    pl.semaphore_wait(barrier, sections - 1 + columns - 1)

    def exchange(source, target, send_sem, recv_sem):
        copies = []
        for d in range(1, sections):
            peer = lax.rem(section + d, sections)
            copy = pltpu.make_async_remote_copy(
                src_ref=source.at[peer],
                dst_ref=target.at[section],
                send_sem=send_sem.at[d],
                recv_sem=recv_sem.at[d],
                device_id={"section": peer},
                device_id_type=MESH,
            )
            copy.start()
            copies.append(copy)
        return copies

    copies1 = exchange(send1, recv1, s1, r1)
    recv1[section] = send1[section]

    for k in range(4):
        by_node = dot(lift_ref[k], const("nodes")[: lift_ref.shape[2]]).astype(bf16)
        wide = dot(const("modes")[:, : lift_ref.shape[1]], by_node).astype(bf16)
        weights[k, :LANE] = wide * const("top")
        weights[k, LANE:] = wide * const("bottom")
    rows_node = const("rows_node")[:, : face_ref.shape[0]]
    face_rows = dot(rows_node, face_ref[...]).astype(bf16)
    face_wide = (dot_nt(face_rows, rows_node) * const("same").astype(f32)).astype(bf16)
    solved[...] = jnp.zeros(solved.shape, f32)
    send3[...] = jnp.zeros(send3.shape, f32)

    for copy in copies1:
        copy.wait()
    factor_copy.wait()

    lane = lax.broadcasted_iota(jnp.int32, (1, LANE), 1)

    def apply_blocks(right, start):
        count = right.shape[0]
        wide = dot(right, const("repeat")).astype(bf16)
        place_row = lax.broadcasted_iota(jnp.int32, (count, chunk * inner), 0) % chunk * inner
        at = lax.broadcasted_iota(jnp.int32, (count, chunk * inner), 1) - place_row
        wide = jnp.where((at >= 0) & (at < inner), wide.astype(f32), 0.0).astype(bf16)
        blocks = []
        for begin in start:
            blocks.append(dot_nt(wide, factor[:, begin : begin + chunk * inner]))
        return blocks

    def work(parts, number, take, metas, ids):
        total = parts * number
        lifted = [None] * parts
        for k in range(4):
            stab[k, :number] = dot(metas[k], const("expand"))
            for c in range(parts):
                traced = take(c, 1 + k)
                shifted = dot(traced, const("shifts"))
                weighted = jnp.zeros((number, LANE), f32)
                for d in range(nvar):
                    weighted += (
                        stab[k, :number, d * LANE : (d + 1) * LANE]
                        * shifted[:, d * LANE : (d + 1) * LANE]
                    )
                pair = split(weighted)
                term = dot_nt(pair, weights[k, LANE:, :LANE])
                term = term[:number] + term[number:]
                lifted[c] = term if k == 0 else lifted[c] + term
                own = dot_nt(pair, face_wide)
                own = own[:number] + own[number:]
                base[k, c * number : (c + 1) * number] = jnp.where(
                    lane < HALF, traced.astype(f32), own
                )
        lifted = [x.astype(bf16) for x in lifted]
        inners = [take(c, 0) for c in range(parts)]
        for begin in range(0, number, chunk):
            cut = slice(begin, begin + chunk)
            rights = [x[cut] for x in inners] + [x[cut] for x in lifted]
            right = jnp.concatenate(rights, axis=0)
            if parts == 1:
                (got,) = apply_blocks(right, [begin * inner])
                for side in range(2):
                    solved[cut, side * LANE : side * LANE + inner] = got[
                        side * chunk : (side + 1) * chunk
                    ]
            else:
                by_real, by_imag = apply_blocks(right, [begin * inner, (number + begin) * inner])
                for side in range(2):
                    a = slice(2 * side * chunk, (2 * side + 1) * chunk)
                    b = slice((2 * side + 1) * chunk, (2 * side + 2) * chunk)
                    lanes = slice(side * LANE, side * LANE + inner)
                    solved[cut, lanes] = by_real[a] - by_imag[b]
                    solved[number + begin : number + begin + chunk, lanes] = by_imag[a] + by_real[b]
        pair = split(solved[:total])
        owner, slot = ids
        rows = columns * 8
        row = lax.broadcasted_iota(jnp.int32, (rows, 1), 0)
        row_col = (row // 8).astype(f32)
        item = row % 8
        index = lax.broadcasted_iota(jnp.int32, (1, number), 1).astype(f32)
        mine = column.astype(f32)
        far = float(8 * col_elems)
        least = jnp.full((rows, 1), far, f32)
        most = jnp.full((rows, 1), -1.0, f32)
        for k in range(4):
            mark = (owner[k : k + 1] == row_col) & (row_col != mine)
            least = jnp.minimum(
                least, jnp.min(jnp.where(mark, index + k * number, far), 1, keepdims=True)
            )
            most = jnp.maximum(
                most, jnp.max(jnp.where(mark, index + k * number, -1.0), 1, keepdims=True)
            )
        wanted = jnp.where(item % 2 == 0, least, jnp.where(most > least, most, -1.0))
        faces = lax.broadcasted_iota(jnp.int32, (col_faces, 1), 0).astype(f32)
        numbers = jnp.zeros((rows, 1), f32)
        items = jnp.zeros((rows, LANE), f32)
        local = [jnp.zeros((col_faces, LANE), f32) for _ in range(parts)]
        for k in range(4):
            mixed = dot(pair, weights[k])
            mixed = mixed[:total] + mixed[total:]
            local_slot = jnp.where(owner[k : k + 1] == mine, slot[k : k + 1], -1.0)
            spread = jnp.where(faces == local_slot, 1.0, 0.0).astype(bf16)
            chosen = jnp.where(index + k * number == wanted, 1.0, 0.0)
            numbers += jnp.sum(chosen * (slot[k : k + 1] + 1.0), 1, keepdims=True)
            for c in range(parts):
                cut = slice(c * number, (c + 1) * number)
                pay = base[k, cut]
                for d in range(nvar):
                    pay -= (
                        stab[k, :number, d * LANE : (d + 1) * LANE]
                        * mixed[cut, d * LANE : (d + 1) * LANE]
                    )
                turned = dot(pay.astype(bf16), const("turns"))
                kind = stab[k, :number, width : width + LANE]
                result = jnp.zeros((number, LANE), f32)
                for place_in, name in enumerate(classes):
                    result = jnp.where(
                        kind == float(name), turned[:, place_in * LANE : (place_in + 1) * LANE], result
                    )
                result = result.astype(bf16)
                local[c] += dot(spread, result)
                picked = jnp.where(item // 2 == c, chosen, 0.0).astype(bf16)
                items += dot(picked, result)
        numbers = jnp.where(item < 2 * parts, numbers - 1.0, -1.0)
        items = jnp.where(lane == HALF - 1, numbers, items)
        send2[...] = items.reshape(columns, 8, LANE)
        for c in range(parts):
            sums[c] = local[c]
        if parts == 1:
            sums[1] = jnp.zeros((col_faces, LANE), f32)

    @pl.when(section == 0)
    def _():
        def take(c, part):
            return jnp.concatenate([recv1[s, part] for s in range(sections)], axis=0)

        ids = ids_ref[...].astype(f32)
        work(1, col_elems, take, [meta_ref[k] for k in range(4)], (ids[:4], ids[4:8] * 16 + ids[8:12]))

    @pl.when(section != 0)
    def _():
        number = sections * third
        r = lax.broadcasted_iota(jnp.int32, (number, col_elems), 0)
        e = lax.broadcasted_iota(jnp.int32, (number, col_elems), 1)
        wanted = r // third * elems + r % third * 3 + (section - 1)
        pick = jnp.where(e == wanted, 1.0, 0.0).astype(bf16)

        def take(c, part):
            return jnp.concatenate(
                [recv1[s, part, c * third : (c + 1) * third] for s in range(sections)], axis=0
            )

        ids = dot_nt(ids_ref[...], pick)
        metas = [dot(pick, meta_ref[k]).astype(bf16) for k in range(4)]
        work(2, number, take, metas, (ids[:4], ids[4:8] * 16 + ids[8:12]))

    def item_copy(d):
        peer = lax.rem(column + d, columns)
        return pltpu.make_async_remote_copy(
            src_ref=send2.at[peer],
            dst_ref=recv2.at[column],
            send_sem=s2.at[d],
            recv_sem=r2.at[d],
            device_id={"elem": peer},
            device_id_type=MESH,
        )

    def start_item(d, carry):
        item_copy(d).start()
        return carry

    def end_item(d, carry):
        item_copy(d).wait()
        return carry

    lax.fori_loop(1, columns, start_item, 0)
    recv2[column] = send2[column]
    lax.fori_loop(1, columns, end_item, 0)
    arrived = recv2[...].reshape(columns * 8, LANE)
    item = lax.broadcasted_iota(jnp.int32, (columns * 8, 1), 0) % 8
    numbers = arrived[:, HALF - 1 : HALF]
    faces = lax.broadcasted_iota(jnp.int32, (1, col_faces), 1).astype(f32)
    for c in range(2):
        hits = jnp.where((numbers == faces) & (item // 2 == c), 1.0, 0.0)
        spread = jnp.transpose(hits).astype(bf16)
        full = sums[c] + dot(spread, arrived.astype(bf16))
        for s in range(sections):
            send3[s, c] = full[s * face_dev : (s + 1) * face_dev]

    copies3 = exchange(send3, recv3, s3, r3)
    recv3[section] = send3[section]
    for copy in copies3:
        copy.wait()
    first = recv3[0, 0]
    second, third_part = recv3[1, 0], recv3[1, 1]
    for s in range(2, sections):
        second += recv3[s, 0]
        third_part += recv3[s, 1]
    for g, total in enumerate((first, second, third_part)):
        out_res[g] = total[:, :face_size]
        out_schur[g] = total[:, HALF : HALF + face_size]


def on_device(
    interior_res,
    face_res,
    trace_vals,
    stabil,
    element_faces,
    orient,
    lift_matrix,
    face_matrix,
    factors,
):
    sections = lax.axis_size("section")
    columns = lax.axis_size("elem")
    elems, inner = interior_res.shape[3:]
    face_size = face_res.shape[5]
    fnodes = face_matrix.shape[0]
    modes = lift_matrix.shape[1]
    nvar = face_size // fnodes
    chunk = 32
    col_elems = sections * elems
    face_dev = 2 * elems
    col_faces = sections * face_dev
    f32, bf16 = jnp.float32, jnp.bfloat16
    consts, place, classes = structure(modes, fnodes, nvar, elems, chunk)

    def widen(x, size):
        return jnp.pad(x, [(0, 0)] * (x.ndim - 1) + [(0, size - x.shape[-1])])

    sides = jnp.concatenate(
        [widen(face_res[:, 0, 0], HALF), widen(trace_vals[:, 0, 0], HALF)], axis=-1
    ).transpose(0, 2, 1, 3)
    pack = jnp.concatenate([widen(interior_res[:, 0], LANE), sides], axis=1)
    meta = jnp.concatenate([stabil[0], orient[0, :, :, :, 1:2].astype(bf16)], axis=-1)
    meta = widen(meta.reshape(col_elems, 4, nvar * nvar + 1).transpose(1, 0, 2), LANE)
    face = element_faces[0].reshape(col_elems, 4).transpose(1, 0)
    slot = face // (face_dev * columns) * face_dev + face % face_dev
    ids = jnp.concatenate(
        [face // face_dev % columns, slot // 16, slot % 16, jnp.zeros_like(slot)], axis=0
    ).astype(bf16)
    dims = (sections, columns, elems, inner, face_size, nvar, chunk)
    out = jax.ShapeDtypeStruct((3, face_dev, face_size), f32)
    vmem = pl.BlockSpec(memory_space=pltpu.VMEM)
    return pl.pallas_call(
        functools.partial(kernel, dims, place, classes),
        out_shape=(out, out),
        in_specs=[vmem] * 6 + [pl.BlockSpec(memory_space=pl.ANY)],
        out_specs=(vmem, vmem),
        scratch_shapes=[
            pltpu.VMEM(factors.shape[2:], bf16),
            pltpu.VMEM((sections, 5, elems, LANE), bf16),
            pltpu.VMEM((sections, 5, elems, LANE), bf16),
            pltpu.VMEM((4, 2 * LANE, nvar * LANE), bf16),
            pltpu.VMEM((4, col_elems, (nvar + 1) * LANE), f32),
            pltpu.VMEM((4, col_elems, LANE), f32),
            pltpu.VMEM((col_elems, 2 * LANE), f32),
            pltpu.VMEM((columns, 8, LANE), f32),
            pltpu.VMEM((columns, 8, LANE), f32),
            pltpu.VMEM((2, col_faces, LANE), f32),
            pltpu.VMEM((sections, 2, face_dev, LANE), f32),
            pltpu.VMEM((sections, 2, face_dev, LANE), f32),
            pltpu.SemaphoreType.DMA,
            pltpu.SemaphoreType.DMA((sections,)),
            pltpu.SemaphoreType.DMA((sections,)),
            pltpu.SemaphoreType.DMA((columns,)),
            pltpu.SemaphoreType.DMA((columns,)),
            pltpu.SemaphoreType.DMA((sections,)),
            pltpu.SemaphoreType.DMA((sections,)),
        ],
        compiler_params=pltpu.CompilerParams(
            collective_id=0, has_side_effects=True, vmem_limit_bytes=56 * 2**20
        ),
    )(pack, meta, ids, lift_matrix, face_matrix, jnp.asarray(consts, bf16), factors)


def solution(mesh):
    return jax.shard_map(
        on_device,
        mesh=mesh,
        in_specs=(
            P(None, "elem", "section", None, None),
            P(None, "elem", "section", None, None, None),
            P(None, "elem", "section", None, None, None),
            P("elem", None, None, None, None),
            P("elem", None, None, None),
            P("elem", None, None, None, None),
            P(),
            P(),
            P("section", "elem", None, None),
        ),
        out_specs=(P(None, ("section", "elem"), None), P(None, ("section", "elem"), None)),
        check_vma=False,
    )
```

```python
import functools

import jax
import jax.numpy as jnp
import numpy as np
from jax import lax
from jax.experimental import pallas as pl
from jax.experimental.pallas import tpu as pltpu
from jax.sharding import PartitionSpec as P

radau_inverse = (
    (4.325579890063155, 0.33919925181580984, 0.5417705399358749),
    (-4.178718591551905, -0.32768282076106237, 0.47662355450055044),
    (-0.5028726349457868, 2.571926949855605, -0.5960392048282249),
)
LANE = 128
HALF = 64
MESH = pl.DeviceIdType.MESH


def triangle_table(fnodes):
    degree = next(d for d in range(1, fnodes) if (d + 1) * (d + 2) // 2 == fnodes)
    lattice = [(a, b, degree - a - b) for a in range(degree + 1) for b in range(degree + 1 - a)]
    rotations = [(0, 1, 2), (1, 2, 0), (2, 0, 1), (0, 2, 1), (2, 1, 0), (1, 0, 2)]
    return [
        [lattice.index(tuple(point[corner] for corner in rotation)) for point in lattice]
        for rotation in rotations
    ]


def structure(modes, fnodes, nvar, elems, chunk):
    lane = np.arange(LANE)
    side, inside = lane // HALF, lane % HALF
    node, var = inside // nvar, inside % nvar
    used = inside < fnodes * nvar
    inner = modes * nvar
    parts, place, at = [], {}, 0

    def add(name, block):
        nonlocal at
        rows, cols = block.shape
        wide = -(-cols // LANE) * LANE
        full = np.zeros((LANE, wide), np.float32)
        full[:rows, :cols] = block
        place[name] = (at, at + wide)
        parts.append(full)
        at += wide

    row = lane[:, None]
    expand, shifts, top, bottom = [], [], [], []
    for d in range(nvar):
        other = (var + d) % nvar
        expand.append((row == (var * nvar + other)[None]) & used[None])
        shifts.append(
            (row == (side * HALF + node * nvar + other)[None]) & (used & (side == 1))[None]
        )
        fit = (row % nvar == other[None]) & used[None] & (row < inner)
        top.append(fit & (side == 0)[None])
        bottom.append(fit & (side == 1)[None])
    add("expand", np.concatenate(expand, 1))
    add("shifts", np.concatenate(shifts, 1))
    add("top", np.concatenate(top, 1))
    add("bottom", np.concatenate(bottom, 1))
    add("modes", (row // nvar == np.arange(modes)[None]) & (row < inner))
    nodes = (np.arange(fnodes)[:, None] == node[None]) & used[None]
    add("nodes", np.concatenate([nodes] * nvar, 1))
    add("rows_node", nodes.T)
    one = used & (side == 1)
    add("same", (var[:, None] == var[None]) & one[:, None] & one[None])
    table = triangle_table(fnodes)
    turns = []
    for order in table:
        order = np.array(order + [0] * HALF)
        source = side * HALF + order[node] * nvar + var
        turns.append((row == source[None]) & used[None])
    add("turns", np.concatenate(turns, 1))
    column = np.arange(chunk * inner)
    add("repeat", row == (column % inner)[None])
    third = elems // 3
    r = np.arange(elems)
    add("thirds", (3 * (r % third) + r // third)[:, None] == r[None])
    return np.concatenate(parts, 1), place, [order[1] for order in table]


def dot(a, b):
    return jnp.dot(a, b, preferred_element_type=jnp.float32)


def dot_nt(a, b):
    return lax.dot_general(a, b, (((1,), (1,)), ((), ())), preferred_element_type=jnp.float32)


def split(x):
    high = x.astype(jnp.bfloat16)
    low = (x - high.astype(jnp.float32)).astype(jnp.bfloat16)
    return jnp.concatenate([high, low], axis=0)


def kernel(
    dims,
    place,
    classes,
    inner_ref,
    face_res_ref,
    trace_ref,
    stabil_ref,
    ids_ref,
    orient_ref,
    lift_ref,
    face_ref,
    const_ref,
    factor_hbm,
    out_res,
    out_schur,
    factor,
    nodal,
    wide_in,
    stab_in,
    lift_in,
    send1,
    recv1,
    weights,
    stab,
    spread_in,
    chosen_in,
    numbers_in,
    base,
    solved,
    send2,
    recv2,
    sums,
    send3,
    recv3,
    factor_sem,
    s1,
    r1,
    s2,
    r2,
    s3,
    r3,
):
    sections, columns, elems, inner, face_size, nvar, chunk = dims
    third = elems // 3
    col_elems = sections * elems
    face_dev = 2 * elems
    col_faces = sections * face_dev
    rows = columns * 8
    f32, bf16 = jnp.float32, jnp.bfloat16
    section = lax.axis_index("section")
    column = lax.axis_index("elem")
    mine = column.astype(f32)

    def const(name):
        lo, hi = place[name]
        return const_ref[:, lo:hi]

    factor_copy = pltpu.make_async_copy(factor_hbm.at[0, 0], factor, factor_sem)
    factor_copy.start()
    barrier = pltpu.get_barrier_semaphore()
    for d in range(1, sections):
        pl.semaphore_signal(
            barrier, inc=1, device_id={"section": lax.rem(section + d, sections)}, device_id_type=MESH
        )

    def greet(d, carry):
        pl.semaphore_signal(
            barrier, inc=1, device_id={"elem": lax.rem(column + d, columns)}, device_id_type=MESH
        )
        return carry

    lax.fori_loop(1, columns, greet, 0)

    send1[...] = jnp.zeros(send1.shape, bf16)
    wide_in[...] = jnp.zeros(wide_in.shape, f32)
    thirds = const("thirds")[:elems, :elems]

    def transformed(values, g):
        row = radau_inverse[g]
        return row[0] * values[0] + row[1] * values[1] + row[2] * values[2]

    for at, source in ((0, face_res_ref), (HALF, trace_ref)):
        values = [source[t].astype(f32) for t in range(3)]
        for g in range(3):
            nodal[g] = transformed(values, g)
        for g in range(3):
            for k in range(4):
                wide_in[g, 1 + k, :, at : at + face_size] = nodal[g, :, k, :]
    values = [inner_ref[t].astype(f32) for t in range(3)]
    for g in range(3):
        wide_in[g, 0, :, :inner] = transformed(values, g)
    for g in range(3):
        for part in range(5):
            w = wide_in[g, part].astype(bf16)
            if g == 0:
                send1[0, part] = w
            else:
                w = dot(thirds, w).astype(bf16)
                for t in range(3):
                    send1[1 + t, part, (g - 1) * third : g * third] = w[t * third : (t + 1) * third]

    pl.semaphore_wait(barrier, sections - 1 + columns - 1)

    def exchange(source, target, send_sem, recv_sem):
        copies = []
        for d in range(1, sections):
            peer = lax.rem(section + d, sections)
            copy = pltpu.make_async_remote_copy(
                src_ref=source.at[peer],
                dst_ref=target.at[section],
                send_sem=send_sem.at[d],
                recv_sem=recv_sem.at[d],
                device_id={"section": peer},
                device_id_type=MESH,
            )
            copy.start()
            copies.append(copy)
        return copies

    copies1 = exchange(send1, recv1, s1, r1)
    recv1[section] = send1[section]

    lift_in[...] = lift_ref[...].astype(f32)
    stab_in[...] = stabil_ref[...].astype(f32)
    for k in range(4):
        lift_k = lift_in[:, k, :].astype(bf16)
        by_mode = dot_nt(const("modes")[:, : lift_ref.shape[2]], lift_k).astype(bf16)
        wide = dot(by_mode, const("nodes")[: lift_ref.shape[0]]).astype(bf16)
        weights[k, :LANE] = wide * const("top")
        weights[k, LANE:] = wide * const("bottom")
    rows_node = const("rows_node")[:, : face_ref.shape[0]]
    face_rows = dot(rows_node, face_ref[...]).astype(bf16)
    face_wide = (dot_nt(face_rows, rows_node) * const("same").astype(f32)).astype(bf16)
    solved[...] = jnp.zeros(solved.shape, f32)
    send3[...] = jnp.zeros(send3.shape, bf16)

    lane = lax.broadcasted_iota(jnp.int32, (1, LANE), 1)
    item = lax.broadcasted_iota(jnp.int32, (rows, 1), 0) % 8

    def prepare(count, step, offset):
        number = sections * count
        r = lax.broadcasted_iota(jnp.int32, (count, elems), 0)
        q = lax.broadcasted_iota(jnp.int32, (count, elems), 1)
        pick = jnp.where(q == step * r + offset, 1.0, 0.0).astype(bf16)
        q = lax.broadcasted_iota(jnp.int32, (elems, number), 0)
        e = lax.broadcasted_iota(jnp.int32, (elems, number), 1)
        names = jnp.zeros((16, number), f32)
        kinds = []
        for s in range(sections):
            face = ids_ref[s].astype(f32)
            strip = jnp.floor((face + 0.5) * (1.0 / face_dev))
            block = jnp.floor((strip + 0.5) * (1.0 / columns))
            slot = block * face_dev + face - strip * face_dev
            high = jnp.floor((slot + 0.5) * (1.0 / 16))
            turn = orient_ref[s, 1].astype(f32)
            table = jnp.concatenate(
                [strip - block * columns, high, slot - 16 * high, jnp.zeros_like(slot)], axis=0
            ).astype(bf16)
            put = jnp.where(q == step * (e - s * count) + offset, 1.0, 0.0).astype(bf16)
            names += dot(table, put)
            kinds.append(dot_nt(pick, turn.astype(bf16)))
        kinds = jnp.concatenate(kinds, axis=0)
        owner, slot = names[:4], 16 * names[4:8] + names[8:12]
        for k in range(4):
            per_block = [
                dot_nt(pick, stab_in[s, :, k, :].astype(bf16)) for s in range(sections)
            ]
            small = jnp.concatenate(per_block, axis=0).astype(bf16)
            stab[k, :number, : nvar * LANE] = dot(small, const("expand")[: nvar * nvar])
            stab[k, :number, nvar * LANE :] = jnp.broadcast_to(kinds[:, k : k + 1], (number, LANE))
        row_col = (lax.broadcasted_iota(jnp.int32, (rows, 1), 0) // 8).astype(f32)
        index = lax.broadcasted_iota(jnp.int32, (1, number), 1).astype(f32)
        far = float(8 * col_elems)
        least = jnp.full((rows, 1), far, f32)
        most = jnp.full((rows, 1), -1.0, f32)
        for k in range(4):
            mark = (owner[k : k + 1] == row_col) & (row_col != mine)
            at = index + k * number
            least = jnp.minimum(least, jnp.min(jnp.where(mark, at, far), 1, keepdims=True))
            most = jnp.maximum(most, jnp.max(jnp.where(mark, at, -1.0), 1, keepdims=True))
        wanted = jnp.where(item % 2 == 0, least, jnp.where(most > least, most, -1.0))
        faces = lax.broadcasted_iota(jnp.int32, (col_faces, 1), 0).astype(f32)
        numbers = jnp.zeros((rows, 1), f32)
        for k in range(4):
            local_slot = jnp.where(owner[k : k + 1] == mine, slot[k : k + 1], -1.0)
            spread_in[k, :, :number] = jnp.where(faces == local_slot, 1.0, 0.0).astype(bf16)
            chosen = jnp.where(index + k * number == wanted, 1.0, 0.0)
            numbers += jnp.sum(chosen * (slot[k : k + 1] + 1.0), 1, keepdims=True)
            chosen_in[k, :, :number] = chosen
        numbers_in[...] = jnp.broadcast_to(numbers - 1.0, (rows, LANE))

    def work(parts, count, take):
        number = sections * count
        total = parts * number
        lifted = [None] * parts
        for k in range(4):
            for c in range(parts):
                traced = take(c, 1 + k)
                shifted = dot(traced, const("shifts"))
                weighted = jnp.zeros((number, LANE), f32)
                for d in range(nvar):
                    weighted += (
                        stab[k, :number, d * LANE : (d + 1) * LANE]
                        * shifted[:, d * LANE : (d + 1) * LANE]
                    )
                pair = split(weighted)
                term = dot_nt(pair, weights[k, LANE:, :LANE])
                term = term[:number] + term[number:]
                lifted[c] = term if k == 0 else lifted[c] + term
                own = dot_nt(pair, face_wide)
                own = own[:number] + own[number:]
                base[k, c * number : (c + 1) * number] = jnp.where(
                    lane < HALF, traced.astype(f32), own
                )
        vectors = [take(c, 0) for c in range(parts)] + [x.astype(bf16) for x in lifted]
        per = len(vectors) * chunk
        begins = list(range(0, number, chunk))
        right = jnp.concatenate([x[b : b + chunk] for b in begins for x in vectors], axis=0)
        reals = [jnp.zeros((per, inner), f32) for _ in begins]
        imags = [jnp.zeros((per, inner), f32) for _ in begins]
        first, span = place["repeat"][0], chunk * inner
        for lo in range(0, span, 512):
            hi = min(lo + 512, span)
            wide = dot(right, const_ref[:, first + lo : first + hi]).astype(bf16)
            r = lax.broadcasted_iota(jnp.int32, (chunk, hi - lo), 0) * inner
            at = lax.broadcasted_iota(jnp.int32, (chunk, hi - lo), 1) + lo - r
            mask = jnp.where((at >= 0) & (at < inner), 1.0, 0.0).astype(bf16)
            wide = wide * jnp.concatenate([mask] * (right.shape[0] // chunk), axis=0)
            for n, b in enumerate(begins):
                cut = wide[n * per : (n + 1) * per]
                reals[n] += dot_nt(cut, factor[:, b * inner + lo : b * inner + hi])
                if parts == 2:
                    at = (number + b) * inner
                    imags[n] += dot_nt(cut, factor[:, at + lo : at + hi])
        for n, b in enumerate(begins):
            for side in range(2):
                lanes = slice(side * LANE, side * LANE + inner)
                one = slice(parts * side * chunk, (parts * side + 1) * chunk)
                if parts == 1:
                    solved[b : b + chunk, lanes] = reals[n][one]
                else:
                    two = slice((2 * side + 1) * chunk, (2 * side + 2) * chunk)
                    solved[b : b + chunk, lanes] = reals[n][one] - imags[n][two]
                    solved[number + b : number + b + chunk, lanes] = imags[n][one] + reals[n][two]
        both = solved[:total].astype(bf16)
        items = jnp.zeros((rows, LANE), f32)
        local = [jnp.zeros((col_faces, LANE), f32) for _ in range(parts)]
        for k in range(4):
            mixed = dot(both, weights[k])
            for c in range(parts):
                cut = slice(c * number, (c + 1) * number)
                pay = base[k, cut]
                for d in range(nvar):
                    pay -= (
                        stab[k, :number, d * LANE : (d + 1) * LANE]
                        * mixed[cut, d * LANE : (d + 1) * LANE]
                    )
                turned = dot(pay.astype(bf16), const("turns"))
                kind = stab[k, :number, nvar * LANE :]
                result = jnp.zeros((number, LANE), f32)
                for n, name in enumerate(classes):
                    result = jnp.where(
                        kind == float(name), turned[:, n * LANE : (n + 1) * LANE], result
                    )
                result = result.astype(bf16)
                local[c] += dot(spread_in[k, :, :number], result)
                picked = jnp.where(item // 2 == c, chosen_in[k, :, :number], 0.0).astype(bf16)
                items += dot(picked, result)
        numbers = jnp.where(item < 2 * parts, numbers_in[...], -1.0)
        items = jnp.where(lane == HALF - 1, numbers, items)
        send2[...] = items.reshape(columns, 8, LANE)
        for c in range(parts):
            sums[c] = local[c]
        if parts == 1:
            sums[1] = jnp.zeros((col_faces, LANE), f32)

    @pl.when(section == 0)
    def _():
        prepare(elems, 1, 0)

    @pl.when(section != 0)
    def _():
        prepare(third, 3, section - 1)

    for copy in copies1:
        copy.wait()
    factor_copy.wait()

    @pl.when(section == 0)
    def _():
        def take(c, part):
            return jnp.concatenate([recv1[s, part] for s in range(sections)], axis=0)

        work(1, elems, take)

    @pl.when(section != 0)
    def _():
        def take(c, part):
            return jnp.concatenate(
                [recv1[s, part, c * third : (c + 1) * third] for s in range(sections)], axis=0
            )

        work(2, third, take)

    def item_copy(d):
        peer = lax.rem(column + d, columns)
        return pltpu.make_async_remote_copy(
            src_ref=send2.at[peer],
            dst_ref=recv2.at[column],
            send_sem=s2.at[d],
            recv_sem=r2.at[d],
            device_id={"elem": peer},
            device_id_type=MESH,
        )

    def start_item(d, carry):
        item_copy(d).start()
        return carry

    def end_item(d, carry):
        item_copy(d).wait()
        return carry

    lax.fori_loop(1, columns, start_item, 0)
    recv2[column] = send2[column]
    lax.fori_loop(1, columns, end_item, 0)
    arrived = recv2[...].reshape(rows, LANE)
    numbers = arrived[:, HALF - 1 : HALF]
    faces = lax.broadcasted_iota(jnp.int32, (1, col_faces), 1).astype(f32)
    for c in range(2):
        hits = jnp.where((numbers == faces) & (item // 2 == c), 1.0, 0.0)
        spread = jnp.transpose(hits).astype(bf16)
        full = (sums[c] + dot(spread, arrived.astype(bf16))).astype(bf16)
        for s in range(sections):
            send3[s, c] = full[s * face_dev : (s + 1) * face_dev]

    copies3 = exchange(send3, recv3, s3, r3)
    recv3[section] = send3[section]
    for copy in copies3:
        copy.wait()
    groups = [(0, 0, 1), (0, 1, sections), (1, 1, sections)]
    for g, (part, begin, end) in enumerate(groups):
        total = recv3[begin, part].astype(f32)
        for s in range(begin + 1, end):
            total += recv3[s, part].astype(f32)
        total = jnp.transpose(total)
        out_res[g] = total[:face_size]
        out_schur[g] = total[HALF : HALF + face_size]


def on_device(
    interior_res,
    face_res,
    trace_vals,
    stabil,
    element_faces,
    orient,
    lift_matrix,
    face_matrix,
    factors,
):
    sections = lax.axis_size("section")
    columns = lax.axis_size("elem")
    elems, inner = interior_res.shape[3:]
    face_size = face_res.shape[5]
    fnodes = face_matrix.shape[0]
    modes = lift_matrix.shape[1]
    nvar = face_size // fnodes
    chunk = 32
    col_elems = sections * elems
    face_dev = 2 * elems
    col_faces = sections * face_dev
    f32, bf16 = jnp.float32, jnp.bfloat16
    consts, place, classes = structure(modes, fnodes, nvar, elems, chunk)

    dims = (sections, columns, elems, inner, face_size, nvar, chunk)
    out = jax.ShapeDtypeStruct((3, face_size, face_dev), f32)
    vmem = pl.BlockSpec(memory_space=pltpu.VMEM)
    residual, schur = pl.pallas_call(
        functools.partial(kernel, dims, place, classes),
        out_shape=(out, out),
        in_specs=[vmem] * 9 + [pl.BlockSpec(memory_space=pl.ANY)],
        out_specs=(vmem, vmem),
        scratch_shapes=[
            pltpu.VMEM(factors.shape[2:], bf16),
            pltpu.VMEM((3, elems, 4, face_size), f32),
            pltpu.VMEM((3, 5, elems, LANE), f32),
            pltpu.VMEM((sections, nvar * nvar, 4, elems), f32),
            pltpu.VMEM((fnodes, 4, modes), f32),
            pltpu.VMEM((sections, 5, elems, LANE), bf16),
            pltpu.VMEM((sections, 5, elems, LANE), bf16),
            pltpu.VMEM((4, 2 * LANE, nvar * LANE), bf16),
            pltpu.VMEM((4, col_elems, (nvar + 1) * LANE), f32),
            pltpu.VMEM((4, col_faces, col_elems), bf16),
            pltpu.VMEM((4, columns * 8, col_elems), f32),
            pltpu.VMEM((columns * 8, LANE), f32),
            pltpu.VMEM((4, col_elems, LANE), f32),
            pltpu.VMEM((col_elems, 2 * LANE), f32),
            pltpu.VMEM((columns, 8, LANE), f32),
            pltpu.VMEM((columns, 8, LANE), f32),
            pltpu.VMEM((2, col_faces, LANE), f32),
            pltpu.VMEM((sections, 2, face_dev, LANE), bf16),
            pltpu.VMEM((sections, 2, face_dev, LANE), bf16),
            pltpu.SemaphoreType.DMA,
            pltpu.SemaphoreType.DMA((sections,)),
            pltpu.SemaphoreType.DMA((sections,)),
            pltpu.SemaphoreType.DMA((columns,)),
            pltpu.SemaphoreType.DMA((columns,)),
            pltpu.SemaphoreType.DMA((sections,)),
            pltpu.SemaphoreType.DMA((sections,)),
        ],
        compiler_params=pltpu.CompilerParams(
            collective_id=0, has_side_effects=True, vmem_limit_bytes=56 * 2**20
        ),
    )(
        interior_res[:, 0, 0],
        face_res[:, 0, 0],
        trace_vals[:, 0, 0],
        stabil[0].transpose(0, 3, 2, 1),
        element_faces[0].transpose(0, 2, 1),
        orient[0].transpose(0, 3, 2, 1),
        lift_matrix.transpose(2, 0, 1),
        face_matrix,
        jnp.asarray(consts, bf16),
        factors,
    )
    return residual.transpose(0, 2, 1), schur.transpose(0, 2, 1)


def solution(mesh):
    return jax.shard_map(
        on_device,
        mesh=mesh,
        in_specs=(
            P(None, "elem", "section", None, None),
            P(None, "elem", "section", None, None, None),
            P(None, "elem", "section", None, None, None),
            P("elem", None, None, None, None),
            P("elem", None, None, None),
            P("elem", None, None, None, None),
            P(),
            P(),
            P("section", "elem", None, None),
        ),
        out_specs=(P(None, ("section", "elem"), None), P(None, ("section", "elem"), None)),
        check_vma=False,
    )
```

```python
import functools

import jax
import jax.numpy as jnp
import numpy as np
from jax import lax
from jax.experimental import pallas as pl
from jax.experimental.pallas import tpu as pltpu
from jax.sharding import PartitionSpec as P

radau_inverse = (
    (4.325579890063155, 0.33919925181580984, 0.5417705399358749),
    (-4.178718591551905, -0.32768282076106237, 0.47662355450055044),
    (-0.5028726349457868, 2.571926949855605, -0.5960392048282249),
)
LANE = 128
HALF = 64
MESH = pl.DeviceIdType.MESH


def triangle_table(fnodes):
    degree = next(d for d in range(1, fnodes) if (d + 1) * (d + 2) // 2 == fnodes)
    lattice = [(a, b, degree - a - b) for a in range(degree + 1) for b in range(degree + 1 - a)]
    rotations = [(0, 1, 2), (1, 2, 0), (2, 0, 1), (0, 2, 1), (2, 1, 0), (1, 0, 2)]
    return [
        [lattice.index(tuple(point[corner] for corner in rotation)) for point in lattice]
        for rotation in rotations
    ]


def structure(modes, fnodes, nvar, chunk):
    lane = np.arange(LANE)
    side, inside = lane // HALF, lane % HALF
    node, var = inside // nvar, inside % nvar
    used = inside < fnodes * nvar
    inner = modes * nvar
    parts, place, at = [], {}, 0

    def add(name, block):
        nonlocal at
        rows, cols = block.shape
        wide = -(-cols // LANE) * LANE
        full = np.zeros((LANE, wide), np.float32)
        full[:rows, :cols] = block
        place[name] = (at, at + wide)
        parts.append(full)
        at += wide

    row = lane[:, None]
    expand, shifts, top, bottom = [], [], [], []
    for d in range(nvar):
        other = (var + d) % nvar
        expand.append((row == (var * nvar + other)[None]) & used[None])
        shifts.append(
            (row == (side * HALF + node * nvar + other)[None]) & (used & (side == 1))[None]
        )
        fit = (row % nvar == other[None]) & used[None] & (row < inner)
        top.append(fit & (side == 0)[None])
        bottom.append(fit & (side == 1)[None])
    add("expand", np.concatenate(expand, 1))
    add("shifts", np.concatenate(shifts, 1))
    add("top", np.concatenate(top, 1))
    add("bottom", np.concatenate(bottom, 1))
    add("modes", (row // nvar == np.arange(modes)[None]) & (row < inner))
    nodes = (np.arange(fnodes)[:, None] == node[None]) & used[None]
    add("nodes", np.concatenate([nodes] * nvar, 1))
    add("rows_node", nodes.T)
    one = used & (side == 1)
    add("same", (var[:, None] == var[None]) & one[:, None] & one[None])
    table = triangle_table(fnodes)
    turns = []
    for order in table:
        order = np.array(order + [0] * HALF)
        source = side * HALF + order[node] * nvar + var
        turns.append((row == source[None]) & used[None])
    add("turns", np.concatenate(turns, 1))
    column = np.arange(chunk * inner)
    add("repeat", row == (column % inner)[None])
    return np.concatenate(parts, 1), place, [order[1] for order in table]


def dot(a, b):
    return jnp.dot(a, b, preferred_element_type=jnp.float32)


def dot_nt(a, b):
    return lax.dot_general(a, b, (((1,), (1,)), ((), ())), preferred_element_type=jnp.float32)


def split(x):
    high = x.astype(jnp.bfloat16)
    low = (x - high.astype(jnp.float32)).astype(jnp.bfloat16)
    return jnp.concatenate([high, low], axis=0)


def kernel(
    dims,
    place,
    classes,
    inner_ref,
    face_res_ref,
    trace_ref,
    stabil_ref,
    ids_ref,
    orient_ref,
    lift_ref,
    face_ref,
    const_hbm,
    factor_hbm,
    out,
    factor,
    const_ref,
    nodal,
    wide_in,
    stab_in,
    lift_in,
    send1,
    recv1,
    weights,
    stab,
    spread_in,
    chosen_in,
    numbers_in,
    base,
    solved,
    send2,
    recv2,
    sums,
    send3,
    recv3,
    factor_sem,
    const_sem,
    s1,
    r1,
    s2,
    r2,
    s3,
    r3,
):
    sections, columns, elems, inner, face_size, nvar, chunk = dims
    third = elems // 3
    col_elems = sections * elems
    face_dev = 2 * elems
    col_faces = sections * face_dev
    rows = columns * 8
    f32, bf16 = jnp.float32, jnp.bfloat16
    section = lax.axis_index("section")
    column = lax.axis_index("elem")
    mine = column.astype(f32)

    def const(name):
        lo, hi = place[name]
        return const_ref[:, lo:hi]

    const_copy = pltpu.make_async_copy(const_hbm, const_ref, const_sem)
    const_copy.start()
    factor_copy = pltpu.make_async_copy(factor_hbm.at[0, 0], factor, factor_sem)
    factor_copy.start()
    barrier = pltpu.get_barrier_semaphore()
    for d in range(1, sections):
        pl.semaphore_signal(
            barrier, inc=1, device_id={"section": lax.rem(section + d, sections)}, device_id_type=MESH
        )

    def greet(d, carry):
        pl.semaphore_signal(
            barrier, inc=1, device_id={"elem": lax.rem(column + d, columns)}, device_id_type=MESH
        )
        return carry

    lax.fori_loop(1, columns, greet, 0)

    send1[...] = jnp.zeros(send1.shape, bf16)
    wide_in[...] = jnp.zeros(wide_in.shape, f32)
    r = lax.broadcasted_iota(jnp.int32, (elems, elems), 0)
    q = lax.broadcasted_iota(jnp.int32, (elems, elems), 1)
    thirds = jnp.where(q == 3 * (r % third) + r // third, 1.0, 0.0).astype(bf16)

    def transformed(values, g):
        row = radau_inverse[g]
        return row[0] * values[0] + row[1] * values[1] + row[2] * values[2]

    for at, source in ((0, face_res_ref), (HALF, trace_ref)):
        values = [source[t].astype(f32) for t in range(3)]
        for g in range(3):
            nodal[g] = transformed(values, g)
        for g in range(3):
            for k in range(4):
                wide_in[g, 1 + k, :, at : at + face_size] = nodal[g, :, k, :]
    values = [inner_ref[t].astype(f32) for t in range(3)]
    for g in range(3):
        wide_in[g, 0, :, :inner] = transformed(values, g)
    for g in range(3):
        for part in range(5):
            w = wide_in[g, part].astype(bf16)
            if g == 0:
                send1[0, part] = w
            else:
                w = dot(thirds, w).astype(bf16)
                for t in range(3):
                    send1[1 + t, part, (g - 1) * third : g * third] = w[t * third : (t + 1) * third]

    pl.semaphore_wait(barrier, sections - 1 + columns - 1)

    def exchange(source, target, send_sem, recv_sem):
        copies = []
        for d in range(1, sections):
            peer = lax.rem(section + d, sections)
            copy = pltpu.make_async_remote_copy(
                src_ref=source.at[peer],
                dst_ref=target.at[section],
                send_sem=send_sem.at[d],
                recv_sem=recv_sem.at[d],
                device_id={"section": peer},
                device_id_type=MESH,
            )
            copy.start()
            copies.append(copy)
        return copies

    copies1 = exchange(send1, recv1, s1, r1)
    recv1[section] = send1[section]
    const_copy.wait()

    lift_in[...] = lift_ref[...].astype(f32)
    stab_in[...] = stabil_ref[...].astype(f32)
    for k in range(4):
        lift_k = lift_in[:, k, :].astype(bf16)
        by_mode = dot_nt(const("modes")[:, : lift_ref.shape[2]], lift_k).astype(bf16)
        wide = dot(by_mode, const("nodes")[: lift_ref.shape[0]]).astype(bf16)
        weights[k, :LANE] = wide * const("top")
        weights[k, LANE:] = wide * const("bottom")
    rows_node = const("rows_node")[:, : face_ref.shape[0]]
    face_rows = dot(rows_node, face_ref[...]).astype(bf16)
    face_wide = (dot_nt(face_rows, rows_node) * const("same").astype(f32)).astype(bf16)
    solved[...] = jnp.zeros(solved.shape, f32)
    send3[...] = jnp.zeros(send3.shape, bf16)

    lane = lax.broadcasted_iota(jnp.int32, (1, LANE), 1)
    item = lax.broadcasted_iota(jnp.int32, (rows, 1), 0) % 8

    def prepare(count, step, offset):
        number = sections * count
        r = lax.broadcasted_iota(jnp.int32, (count, elems), 0)
        q = lax.broadcasted_iota(jnp.int32, (count, elems), 1)
        pick = jnp.where(q == step * r + offset, 1.0, 0.0).astype(bf16)
        q = lax.broadcasted_iota(jnp.int32, (elems, number), 0)
        e = lax.broadcasted_iota(jnp.int32, (elems, number), 1)
        names = jnp.zeros((16, number), f32)
        kinds = []
        for s in range(sections):
            face = ids_ref[s].astype(f32)
            strip = jnp.floor((face + 0.5) * (1.0 / face_dev))
            block = jnp.floor((strip + 0.5) * (1.0 / columns))
            slot = block * face_dev + face - strip * face_dev
            high = jnp.floor((slot + 0.5) * (1.0 / 16))
            turn = orient_ref[s, 1].astype(f32)
            table = jnp.concatenate(
                [strip - block * columns, high, slot - 16 * high, jnp.zeros_like(slot)], axis=0
            ).astype(bf16)
            put = jnp.where(q == step * (e - s * count) + offset, 1.0, 0.0).astype(bf16)
            names += dot(table, put)
            kinds.append(dot_nt(pick, turn.astype(bf16)))
        kinds = jnp.concatenate(kinds, axis=0)
        owner, slot = names[:4], 16 * names[4:8] + names[8:12]
        for k in range(4):
            per_block = [
                dot_nt(pick, stab_in[s, :, k, :].astype(bf16)) for s in range(sections)
            ]
            small = jnp.concatenate(per_block, axis=0).astype(bf16)
            stab[k, :number, : nvar * LANE] = dot(small, const("expand")[: nvar * nvar])
            stab[k, :number, nvar * LANE :] = jnp.broadcast_to(kinds[:, k : k + 1], (number, LANE))
        row_col = (lax.broadcasted_iota(jnp.int32, (rows, 1), 0) // 8).astype(f32)
        index = lax.broadcasted_iota(jnp.int32, (1, number), 1).astype(f32)
        far = float(8 * col_elems)
        least = jnp.full((rows, 1), far, f32)
        most = jnp.full((rows, 1), -1.0, f32)
        for k in range(4):
            mark = (owner[k : k + 1] == row_col) & (row_col != mine)
            at = index + k * number
            least = jnp.minimum(least, jnp.min(jnp.where(mark, at, far), 1, keepdims=True))
            most = jnp.maximum(most, jnp.max(jnp.where(mark, at, -1.0), 1, keepdims=True))
        wanted = jnp.where(item % 2 == 0, least, jnp.where(most > least, most, -1.0))
        faces = lax.broadcasted_iota(jnp.int32, (col_faces, 1), 0).astype(f32)
        numbers = jnp.zeros((rows, 1), f32)
        for k in range(4):
            local_slot = jnp.where(owner[k : k + 1] == mine, slot[k : k + 1], -1.0)
            spread_in[k, :, :number] = jnp.where(faces == local_slot, 1.0, 0.0).astype(bf16)
            chosen = jnp.where(index + k * number == wanted, 1.0, 0.0)
            numbers += jnp.sum(chosen * (slot[k : k + 1] + 1.0), 1, keepdims=True)
            chosen_in[k, :, :number] = chosen
        numbers_in[...] = jnp.broadcast_to(numbers - 1.0, (rows, LANE))

    def work(parts, count, take):
        number = sections * count
        total = parts * number
        lifted = [None] * parts
        for k in range(4):
            for c in range(parts):
                traced = take(c, 1 + k)
                shifted = dot(traced, const("shifts"))
                weighted = jnp.zeros((number, LANE), f32)
                for d in range(nvar):
                    weighted += (
                        stab[k, :number, d * LANE : (d + 1) * LANE]
                        * shifted[:, d * LANE : (d + 1) * LANE]
                    )
                pair = split(weighted)
                term = dot_nt(pair, weights[k, LANE:, :LANE])
                term = term[:number] + term[number:]
                lifted[c] = term if k == 0 else lifted[c] + term
                own = dot_nt(pair, face_wide)
                own = own[:number] + own[number:]
                base[k, c * number : (c + 1) * number] = jnp.where(
                    lane < HALF, traced.astype(f32), own
                )
        vectors = [take(c, 0) for c in range(parts)] + [x.astype(bf16) for x in lifted]
        per = len(vectors) * chunk
        begins = list(range(0, number, chunk))
        right = jnp.concatenate([x[b : b + chunk] for b in begins for x in vectors], axis=0)
        reals = [jnp.zeros((per, inner), f32) for _ in begins]
        imags = [jnp.zeros((per, inner), f32) for _ in begins]
        first, span = place["repeat"][0], chunk * inner
        for lo in range(0, span, 512):
            hi = min(lo + 512, span)
            wide = dot(right, const_ref[:, first + lo : first + hi]).astype(bf16)
            r = lax.broadcasted_iota(jnp.int32, (chunk, hi - lo), 0) * inner
            at = lax.broadcasted_iota(jnp.int32, (chunk, hi - lo), 1) + lo - r
            mask = jnp.where((at >= 0) & (at < inner), 1.0, 0.0).astype(bf16)
            wide = wide * jnp.concatenate([mask] * (right.shape[0] // chunk), axis=0)
            for n, b in enumerate(begins):
                cut = wide[n * per : (n + 1) * per]
                reals[n] += dot_nt(cut, factor[:, b * inner + lo : b * inner + hi])
                if parts == 2:
                    at = (number + b) * inner
                    imags[n] += dot_nt(cut, factor[:, at + lo : at + hi])
        for n, b in enumerate(begins):
            for side in range(2):
                lanes = slice(side * LANE, side * LANE + inner)
                one = slice(parts * side * chunk, (parts * side + 1) * chunk)
                if parts == 1:
                    solved[b : b + chunk, lanes] = reals[n][one]
                else:
                    two = slice((2 * side + 1) * chunk, (2 * side + 2) * chunk)
                    solved[b : b + chunk, lanes] = reals[n][one] - imags[n][two]
                    solved[number + b : number + b + chunk, lanes] = imags[n][one] + reals[n][two]
        both = solved[:total].astype(bf16)
        items = jnp.zeros((rows, LANE), f32)
        local = [jnp.zeros((col_faces, LANE), f32) for _ in range(parts)]
        for k in range(4):
            mixed = dot(both, weights[k])
            for c in range(parts):
                cut = slice(c * number, (c + 1) * number)
                pay = base[k, cut]
                for d in range(nvar):
                    pay -= (
                        stab[k, :number, d * LANE : (d + 1) * LANE]
                        * mixed[cut, d * LANE : (d + 1) * LANE]
                    )
                turned = dot(pay.astype(bf16), const("turns"))
                kind = stab[k, :number, nvar * LANE :]
                result = jnp.zeros((number, LANE), f32)
                for n, name in enumerate(classes):
                    result = jnp.where(
                        kind == float(name), turned[:, n * LANE : (n + 1) * LANE], result
                    )
                result = result.astype(bf16)
                local[c] += dot(spread_in[k, :, :number], result)
                picked = jnp.where(item // 2 == c, chosen_in[k, :, :number], 0.0).astype(bf16)
                items += dot(picked, result)
        numbers = jnp.where(item < 2 * parts, numbers_in[...], -1.0)
        items = jnp.where(lane == HALF - 1, numbers, items)
        send2[...] = items.reshape(columns, 8, LANE)
        for c in range(parts):
            sums[c] = local[c]
        if parts == 1:
            sums[1] = jnp.zeros((col_faces, LANE), f32)

    @pl.when(section == 0)
    def _():
        prepare(elems, 1, 0)

    @pl.when(section != 0)
    def _():
        prepare(third, 3, section - 1)

    for copy in copies1:
        copy.wait()
    factor_copy.wait()

    @pl.when(section == 0)
    def _():
        def take(c, part):
            return jnp.concatenate([recv1[s, part] for s in range(sections)], axis=0)

        work(1, elems, take)

    @pl.when(section != 0)
    def _():
        def take(c, part):
            return jnp.concatenate(
                [recv1[s, part, c * third : (c + 1) * third] for s in range(sections)], axis=0
            )

        work(2, third, take)

    def item_copy(d):
        peer = lax.rem(column + d, columns)
        return pltpu.make_async_remote_copy(
            src_ref=send2.at[peer],
            dst_ref=recv2.at[column],
            send_sem=s2.at[d],
            recv_sem=r2.at[d],
            device_id={"elem": peer},
            device_id_type=MESH,
        )

    def start_item(d, carry):
        item_copy(d).start()
        return carry

    def end_item(d, carry):
        item_copy(d).wait()
        return carry

    lax.fori_loop(1, columns, start_item, 0)
    recv2[column] = send2[column]
    lax.fori_loop(1, columns, end_item, 0)
    arrived = recv2[...].reshape(rows, LANE)
    numbers = arrived[:, HALF - 1 : HALF]
    faces = lax.broadcasted_iota(jnp.int32, (1, col_faces), 1).astype(f32)
    for c in range(2):
        hits = jnp.where((numbers == faces) & (item // 2 == c), 1.0, 0.0)
        spread = jnp.transpose(hits).astype(bf16)
        full = (sums[c] + dot(spread, arrived.astype(bf16))).astype(bf16)
        for s in range(sections):
            send3[s, c] = full[s * face_dev : (s + 1) * face_dev]

    copies3 = exchange(send3, recv3, s3, r3)
    recv3[section] = send3[section]
    for copy in copies3:
        copy.wait()
    groups = [(0, 0, 1), (0, 1, sections), (1, 1, sections)]
    for g, (part, begin, end) in enumerate(groups):
        total = recv3[begin, part].astype(f32)
        for s in range(begin + 1, end):
            total += recv3[s, part].astype(f32)
        out[g] = jnp.transpose(total)


def part_sides(face_size, both, out_res, out_schur):
    out_res[...] = both[:, :face_size]
    out_schur[...] = both[:, HALF : HALF + face_size]


def on_device(
    interior_res,
    face_res,
    trace_vals,
    stabil,
    element_faces,
    orient,
    lift_matrix,
    face_matrix,
    factors,
):
    sections = lax.axis_size("section")
    columns = lax.axis_size("elem")
    elems, inner = interior_res.shape[3:]
    face_size = face_res.shape[5]
    fnodes = face_matrix.shape[0]
    modes = lift_matrix.shape[1]
    nvar = face_size // fnodes
    chunk = 32
    col_elems = sections * elems
    face_dev = 2 * elems
    col_faces = sections * face_dev
    f32, bf16 = jnp.float32, jnp.bfloat16
    consts, place, classes = structure(modes, fnodes, nvar, chunk)

    dims = (sections, columns, elems, inner, face_size, nvar, chunk)
    out = jax.ShapeDtypeStruct((3, face_size, face_dev), f32)
    vmem = pl.BlockSpec(memory_space=pltpu.VMEM)
    both = pl.pallas_call(
        functools.partial(kernel, dims, place, classes),
        out_shape=jax.ShapeDtypeStruct((3, LANE, face_dev), f32),
        in_specs=[vmem] * 8 + [pl.BlockSpec(memory_space=pl.ANY)] * 2,
        out_specs=vmem,
        scratch_shapes=[
            pltpu.VMEM(factors.shape[2:], bf16),
            pltpu.VMEM(consts.shape, bf16),
            pltpu.VMEM((3, elems, 4, face_size), f32),
            pltpu.VMEM((3, 5, elems, LANE), f32),
            pltpu.VMEM((sections, nvar * nvar, 4, elems), f32),
            pltpu.VMEM((fnodes, 4, modes), f32),
            pltpu.VMEM((sections, 5, elems, LANE), bf16),
            pltpu.VMEM((sections, 5, elems, LANE), bf16),
            pltpu.VMEM((4, 2 * LANE, nvar * LANE), bf16),
            pltpu.VMEM((4, col_elems, (nvar + 1) * LANE), f32),
            pltpu.VMEM((4, col_faces, col_elems), bf16),
            pltpu.VMEM((4, columns * 8, col_elems), f32),
            pltpu.VMEM((columns * 8, LANE), f32),
            pltpu.VMEM((4, col_elems, LANE), f32),
            pltpu.VMEM((col_elems, 2 * LANE), f32),
            pltpu.VMEM((columns, 8, LANE), f32),
            pltpu.VMEM((columns, 8, LANE), f32),
            pltpu.VMEM((2, col_faces, LANE), f32),
            pltpu.VMEM((sections, 2, face_dev, LANE), bf16),
            pltpu.VMEM((sections, 2, face_dev, LANE), bf16),
            pltpu.SemaphoreType.DMA,
            pltpu.SemaphoreType.DMA,
            pltpu.SemaphoreType.DMA((sections,)),
            pltpu.SemaphoreType.DMA((sections,)),
            pltpu.SemaphoreType.DMA((columns,)),
            pltpu.SemaphoreType.DMA((columns,)),
            pltpu.SemaphoreType.DMA((sections,)),
            pltpu.SemaphoreType.DMA((sections,)),
        ],
        compiler_params=pltpu.CompilerParams(
            collective_id=0, has_side_effects=True, vmem_limit_bytes=56 * 2**20
        ),
    )(
        interior_res[:, 0, 0],
        face_res[:, 0, 0],
        trace_vals[:, 0, 0],
        stabil[0].transpose(0, 3, 2, 1),
        element_faces[0].transpose(0, 2, 1),
        orient[0].transpose(0, 3, 2, 1),
        lift_matrix.transpose(2, 0, 1),
        face_matrix,
        jnp.asarray(consts, bf16),
        factors,
    )
    residual, schur = pl.pallas_call(
        functools.partial(part_sides, face_size),
        out_shape=(out, out),
        in_specs=[vmem],
        out_specs=(vmem, vmem),
    )(both)
    return residual.transpose(0, 2, 1), schur.transpose(0, 2, 1)


def solution(mesh):
    return jax.shard_map(
        on_device,
        mesh=mesh,
        in_specs=(
            P(None, "elem", "section", None, None),
            P(None, "elem", "section", None, None, None),
            P(None, "elem", "section", None, None, None),
            P("elem", None, None, None, None),
            P("elem", None, None, None),
            P("elem", None, None, None, None),
            P(),
            P(),
            P("section", "elem", None, None),
        ),
        out_specs=(P(None, ("section", "elem"), None), P(None, ("section", "elem"), None)),
        check_vma=False,
    )
```

```python
import functools

import jax
import jax.numpy as jnp
import numpy as np
from jax import lax
from jax.experimental import pallas as pl
from jax.experimental.pallas import tpu as pltpu
from jax.sharding import PartitionSpec as P

radau_inverse = (
    (4.325579890063155, 0.33919925181580984, 0.5417705399358749),
    (-4.178718591551905, -0.32768282076106237, 0.47662355450055044),
    (-0.5028726349457868, 2.571926949855605, -0.5960392048282249),
)
LANE = 128
HALF = 64
MESH = pl.DeviceIdType.MESH


def triangle_table(fnodes):
    degree = next(d for d in range(1, fnodes) if (d + 1) * (d + 2) // 2 == fnodes)
    lattice = [(a, b, degree - a - b) for a in range(degree + 1) for b in range(degree + 1 - a)]
    rotations = [(0, 1, 2), (1, 2, 0), (2, 0, 1), (0, 2, 1), (2, 1, 0), (1, 0, 2)]
    return [
        [lattice.index(tuple(point[corner] for corner in rotation)) for point in lattice]
        for rotation in rotations
    ]


def structure(modes, fnodes, nvar, chunk):
    lane = np.arange(LANE)
    side, inside = lane // HALF, lane % HALF
    node, var = inside // nvar, inside % nvar
    used = inside < fnodes * nvar
    inner = modes * nvar
    parts, place, at = [], {}, 0

    def add(name, block):
        nonlocal at
        rows, cols = block.shape
        wide = -(-cols // LANE) * LANE
        full = np.zeros((LANE, wide), np.float32)
        full[:rows, :cols] = block
        place[name] = (at, at + wide)
        parts.append(full)
        at += wide

    row = lane[:, None]
    expand, shifts, top, bottom = [], [], [], []
    for d in range(nvar):
        other = (var + d) % nvar
        expand.append((row == (var * nvar + other)[None]) & used[None])
        shifts.append(
            (row == (side * HALF + node * nvar + other)[None]) & (used & (side == 1))[None]
        )
        fit = (row % nvar == other[None]) & used[None] & (row < inner)
        top.append(fit & (side == 0)[None])
        bottom.append(fit & (side == 1)[None])
    add("expand", np.concatenate(expand, 1))
    add("shifts", np.concatenate(shifts, 1))
    add("top", np.concatenate(top, 1))
    add("bottom", np.concatenate(bottom, 1))
    add("modes", (row // nvar == np.arange(modes)[None]) & (row < inner))
    nodes = (np.arange(fnodes)[:, None] == node[None]) & used[None]
    add("nodes", np.concatenate([nodes] * nvar, 1))
    add("rows_node", nodes.T)
    one = used & (side == 1)
    add("same", (var[:, None] == var[None]) & one[:, None] & one[None])
    table = triangle_table(fnodes)
    turns = []
    for order in table:
        order = np.array(order + [0] * HALF)
        source = side * HALF + order[node] * nvar + var
        turns.append((row == source[None]) & used[None])
    add("turns", np.concatenate(turns, 1))
    column = np.arange(chunk * inner)
    add("repeat", row == (column % inner)[None])
    return np.concatenate(parts, 1), place, [order[1] for order in table]


def dot(a, b):
    return jnp.dot(a, b, preferred_element_type=jnp.float32)


def dot_nt(a, b):
    return lax.dot_general(a, b, (((1,), (1,)), ((), ())), preferred_element_type=jnp.float32)


def split(x):
    high = x.astype(jnp.bfloat16)
    low = (x - high.astype(jnp.float32)).astype(jnp.bfloat16)
    return jnp.concatenate([high, low], axis=0)


def kernel(
    dims,
    place,
    classes,
    inner_ref,
    face_res_ref,
    trace_ref,
    stabil_ref,
    ids_ref,
    orient_ref,
    lift_ref,
    face_ref,
    const_hbm,
    factor_hbm,
    out,
    factor,
    const_ref,
    nodal,
    wide_in,
    stab_in,
    lift_in,
    send1,
    recv1,
    weights,
    stab,
    spread_in,
    chosen_in,
    numbers_in,
    base,
    solved,
    send2,
    recv2,
    send3,
    recv3,
    factor_sem,
    const_sem,
    s1,
    r1,
    s2,
    r2,
    s3,
    r3,
):
    sections, columns, elems, inner, face_size, nvar, chunk = dims
    third = elems // 3
    col_elems = sections * elems
    face_dev = 2 * elems
    col_faces = sections * face_dev
    rows = columns * 8
    f32, bf16 = jnp.float32, jnp.bfloat16
    section = lax.axis_index("section")
    column = lax.axis_index("elem")
    mine = column.astype(f32)

    def const(name):
        lo, hi = place[name]
        return const_ref[:, lo:hi]

    const_copy = pltpu.make_async_copy(const_hbm, const_ref, const_sem)
    const_copy.start()
    factor_copy = pltpu.make_async_copy(factor_hbm.at[0, 0], factor, factor_sem)
    factor_copy.start()
    barrier = pltpu.get_barrier_semaphore()
    def device(step, d):
        return {
            "section": lax.rem(section + step, sections),
            "elem": lax.rem(column + d, columns),
        }

    for step in range(sections):

        def greet(d, carry):
            pl.semaphore_signal(barrier, inc=1, device_id=device(step, d), device_id_type=MESH)
            return carry

        lax.fori_loop(int(step == 0), columns, greet, 0)

    send1[...] = jnp.zeros(send1.shape, bf16)
    wide_in[...] = jnp.zeros(wide_in.shape, f32)
    r = lax.broadcasted_iota(jnp.int32, (elems, elems), 0)
    q = lax.broadcasted_iota(jnp.int32, (elems, elems), 1)
    thirds = jnp.where(q == 3 * (r % third) + r // third, 1.0, 0.0).astype(bf16)

    def transformed(values, g):
        row = radau_inverse[g]
        return row[0] * values[0] + row[1] * values[1] + row[2] * values[2]

    for at, source in ((0, face_res_ref), (HALF, trace_ref)):
        values = [source[t].astype(f32) for t in range(3)]
        for g in range(3):
            nodal[g] = transformed(values, g)
        for g in range(3):
            for k in range(4):
                wide_in[g, 1 + k, :, at : at + face_size] = nodal[g, :, k, :]
    values = [inner_ref[t].astype(f32) for t in range(3)]
    for g in range(3):
        wide_in[g, 0, :, :inner] = transformed(values, g)
    for g in range(3):
        for part in range(5):
            w = wide_in[g, part].astype(bf16)
            if g == 0:
                send1[0, part] = w
            else:
                w = dot(thirds, w).astype(bf16)
                for t in range(3):
                    send1[1 + t, part, (g - 1) * third : g * third] = w[t * third : (t + 1) * third]

    pl.semaphore_wait(barrier, sections * columns - 1)

    def exchange(source, target, send_sem, recv_sem):
        copies = []
        for d in range(1, sections):
            peer = lax.rem(section + d, sections)
            copy = pltpu.make_async_remote_copy(
                src_ref=source.at[peer],
                dst_ref=target.at[section],
                send_sem=send_sem.at[d],
                recv_sem=recv_sem.at[d],
                device_id={"section": peer},
                device_id_type=MESH,
            )
            copy.start()
            copies.append(copy)
        return copies

    copies1 = exchange(send1, recv1, s1, r1)
    recv1[section] = send1[section]
    const_copy.wait()

    lift_in[...] = lift_ref[...].astype(f32)
    stab_in[...] = stabil_ref[...].astype(f32)
    for k in range(4):
        lift_k = lift_in[:, k, :].astype(bf16)
        by_mode = dot_nt(const("modes")[:, : lift_ref.shape[2]], lift_k).astype(bf16)
        wide = dot(by_mode, const("nodes")[: lift_ref.shape[0]]).astype(bf16)
        weights[k, :LANE] = wide * const("top")
        weights[k, LANE:] = wide * const("bottom")
    rows_node = const("rows_node")[:, : face_ref.shape[0]]
    face_rows = dot(rows_node, face_ref[...]).astype(bf16)
    face_wide = (dot_nt(face_rows, rows_node) * const("same").astype(f32)).astype(bf16)
    solved[...] = jnp.zeros(solved.shape, f32)
    send3[...] = jnp.zeros(send3.shape, bf16)

    lane = lax.broadcasted_iota(jnp.int32, (1, LANE), 1)
    item = lax.broadcasted_iota(jnp.int32, (rows, 1), 0) % 8

    def prepare(count, step, offset):
        number = sections * count
        r = lax.broadcasted_iota(jnp.int32, (count, elems), 0)
        q = lax.broadcasted_iota(jnp.int32, (count, elems), 1)
        pick = jnp.where(q == step * r + offset, 1.0, 0.0).astype(bf16)
        q = lax.broadcasted_iota(jnp.int32, (elems, number), 0)
        e = lax.broadcasted_iota(jnp.int32, (elems, number), 1)
        names = jnp.zeros((16, number), f32)
        kinds = []
        for s in range(sections):
            face = ids_ref[s].astype(f32)
            strip = jnp.floor((face + 0.5) * (1.0 / face_dev))
            block = jnp.floor((strip + 0.5) * (1.0 / columns))
            slot = block * face_dev + face - strip * face_dev
            high = jnp.floor((slot + 0.5) * (1.0 / 16))
            turn = orient_ref[s, 1].astype(f32)
            table = jnp.concatenate(
                [strip - block * columns, high, slot - 16 * high, jnp.zeros_like(slot)], axis=0
            ).astype(bf16)
            put = jnp.where(q == step * (e - s * count) + offset, 1.0, 0.0).astype(bf16)
            names += dot(table, put)
            kinds.append(dot_nt(pick, turn.astype(bf16)))
        kinds = jnp.concatenate(kinds, axis=0)
        owner, slot = names[:4], 16 * names[4:8] + names[8:12]
        for k in range(4):
            per_block = [
                dot_nt(pick, stab_in[s, :, k, :].astype(bf16)) for s in range(sections)
            ]
            small = jnp.concatenate(per_block, axis=0).astype(bf16)
            stab[k, :number, : nvar * LANE] = dot(small, const("expand")[: nvar * nvar])
            stab[k, :number, nvar * LANE :] = jnp.broadcast_to(kinds[:, k : k + 1], (number, LANE))
        row_col = (lax.broadcasted_iota(jnp.int32, (rows, 1), 0) // 8).astype(f32)
        index = lax.broadcasted_iota(jnp.int32, (1, number), 1).astype(f32)
        far = float(8 * col_elems)
        least = jnp.full((rows, 1), far, f32)
        most = jnp.full((rows, 1), -1.0, f32)
        for k in range(4):
            mark = (owner[k : k + 1] == row_col) & (row_col != mine)
            at = index + k * number
            least = jnp.minimum(least, jnp.min(jnp.where(mark, at, far), 1, keepdims=True))
            most = jnp.maximum(most, jnp.max(jnp.where(mark, at, -1.0), 1, keepdims=True))
        wanted = jnp.where(item % 2 == 0, least, jnp.where(most > least, most, -1.0))
        faces = lax.broadcasted_iota(jnp.int32, (col_faces, 1), 0).astype(f32)
        numbers = jnp.zeros((rows, 1), f32)
        for k in range(4):
            local_slot = jnp.where(owner[k : k + 1] == mine, slot[k : k + 1], -1.0)
            spread_in[k, :, :number] = jnp.where(faces == local_slot, 1.0, 0.0).astype(bf16)
            chosen = jnp.where(index + k * number == wanted, 1.0, 0.0)
            numbers += jnp.sum(chosen * (slot[k : k + 1] + 1.0), 1, keepdims=True)
            chosen_in[k, :, :number] = chosen
        numbers_in[...] = jnp.broadcast_to(numbers - 1.0, (rows, LANE))

    def work(parts, count, take):
        number = sections * count
        total = parts * number
        lifted = [None] * parts
        for k in range(4):
            for c in range(parts):
                traced = take(c, 1 + k)
                shifted = dot(traced, const("shifts"))
                weighted = jnp.zeros((number, LANE), f32)
                for d in range(nvar):
                    weighted += (
                        stab[k, :number, d * LANE : (d + 1) * LANE]
                        * shifted[:, d * LANE : (d + 1) * LANE]
                    )
                pair = split(weighted)
                term = dot_nt(pair, weights[k, LANE:, :LANE])
                term = term[:number] + term[number:]
                lifted[c] = term if k == 0 else lifted[c] + term
                own = dot_nt(pair, face_wide)
                own = own[:number] + own[number:]
                base[k, c * number : (c + 1) * number] = jnp.where(
                    lane < HALF, traced.astype(f32), own
                )
        vectors = [take(c, 0) for c in range(parts)] + [x.astype(bf16) for x in lifted]
        per = len(vectors) * chunk
        begins = list(range(0, number, chunk))
        right = jnp.concatenate([x[b : b + chunk] for b in begins for x in vectors], axis=0)
        reals = [jnp.zeros((per, inner), f32) for _ in begins]
        imags = [jnp.zeros((per, inner), f32) for _ in begins]
        first, span = place["repeat"][0], chunk * inner
        for lo in range(0, span, 512):
            hi = min(lo + 512, span)
            wide = dot(right, const_ref[:, first + lo : first + hi]).astype(bf16)
            r = lax.broadcasted_iota(jnp.int32, (chunk, hi - lo), 0) * inner
            at = lax.broadcasted_iota(jnp.int32, (chunk, hi - lo), 1) + lo - r
            mask = jnp.where((at >= 0) & (at < inner), 1.0, 0.0).astype(bf16)
            wide = wide * jnp.concatenate([mask] * (right.shape[0] // chunk), axis=0)
            for n, b in enumerate(begins):
                cut = wide[n * per : (n + 1) * per]
                reals[n] += dot_nt(cut, factor[:, b * inner + lo : b * inner + hi])
                if parts == 2:
                    at = (number + b) * inner
                    imags[n] += dot_nt(cut, factor[:, at + lo : at + hi])
        for n, b in enumerate(begins):
            for side in range(2):
                lanes = slice(side * LANE, side * LANE + inner)
                one = slice(parts * side * chunk, (parts * side + 1) * chunk)
                if parts == 1:
                    solved[b : b + chunk, lanes] = reals[n][one]
                else:
                    two = slice((2 * side + 1) * chunk, (2 * side + 2) * chunk)
                    solved[b : b + chunk, lanes] = reals[n][one] - imags[n][two]
                    solved[number + b : number + b + chunk, lanes] = imags[n][one] + reals[n][two]
        both = solved[:total].astype(bf16)
        items = jnp.zeros((rows, LANE), f32)
        local = [jnp.zeros((col_faces, LANE), f32) for _ in range(parts)]
        for k in range(4):
            mixed = dot(both, weights[k])
            for c in range(parts):
                cut = slice(c * number, (c + 1) * number)
                pay = base[k, cut]
                for d in range(nvar):
                    pay -= (
                        stab[k, :number, d * LANE : (d + 1) * LANE]
                        * mixed[cut, d * LANE : (d + 1) * LANE]
                    )
                turned = dot(pay.astype(bf16), const("turns"))
                kind = stab[k, :number, nvar * LANE :]
                result = jnp.zeros((number, LANE), f32)
                for n, name in enumerate(classes):
                    result = jnp.where(
                        kind == float(name), turned[:, n * LANE : (n + 1) * LANE], result
                    )
                result = result.astype(bf16)
                local[c] += dot(spread_in[k, :, :number], result)
                picked = jnp.where(item // 2 == c, chosen_in[k, :, :number], 0.0).astype(bf16)
                items += dot(picked, result)
        numbers = jnp.where(item < 2 * parts, numbers_in[...], -1.0)
        items = jnp.where(lane == HALF - 1, numbers, items)
        send2[...] = items.reshape(columns, 8, LANE)
        for c in range(parts):
            full = local[c].astype(bf16)
            for s in range(sections):
                send3[s, c] = full[s * face_dev : (s + 1) * face_dev]

    @pl.when(section == 0)
    def _():
        prepare(elems, 1, 0)

    @pl.when(section != 0)
    def _():
        prepare(third, 3, section - 1)

    for copy in copies1:
        copy.wait()
    factor_copy.wait()

    @pl.when(section == 0)
    def _():
        def take(c, part):
            return jnp.concatenate([recv1[s, part] for s in range(sections)], axis=0)

        work(1, elems, take)

    @pl.when(section != 0)
    def _():
        def take(c, part):
            return jnp.concatenate(
                [recv1[s, part, c * third : (c + 1) * third] for s in range(sections)], axis=0
            )

        work(2, third, take)

    copies3 = exchange(send3, recv3, s3, r3)

    def item_copy(step, d):
        peer = device(step, d)
        return pltpu.make_async_remote_copy(
            src_ref=send2.at[peer["elem"]],
            dst_ref=recv2.at[section, column],
            send_sem=s2.at[step * columns + d],
            recv_sem=r2.at[step * columns + d],
            device_id=peer,
            device_id_type=MESH,
        )

    for step in range(sections):

        def start_item(d, carry):
            item_copy(step, d).start()
            return carry

        lax.fori_loop(1, columns, start_item, 0)
    recv3[section] = send3[section]
    for step in range(sections):

        def end_item(d, carry):
            item_copy(step, d).wait()
            return carry

        lax.fori_loop(1, columns, end_item, 0)

    r = lax.broadcasted_iota(jnp.int32, (sections * rows, 1), 0)
    own = (r % rows) // 8 == column
    kind, origin = (r % 8) // 2, r // rows
    arrived = jnp.where(own, 0.0, recv2[...].reshape(sections * rows, LANE))
    numbers = jnp.where(own, -1.0, arrived[:, HALF - 1 : HALF])
    numbers -= (section * face_dev).astype(f32)
    arrived = jnp.transpose(arrived).astype(bf16)
    faces = lax.broadcasted_iota(jnp.int32, (1, face_dev), 1).astype(f32)
    groups = [(0, 0, 1), (0, 1, sections), (1, 1, sections)]
    extra = []
    for part, begin, end in groups:
        meant = (kind == part) & (origin >= begin) & (origin < end)
        hits = jnp.where((numbers == faces) & meant, 1.0, 0.0).astype(bf16)
        extra.append(dot(arrived, hits))
    for copy in copies3:
        copy.wait()
    for g, (part, begin, end) in enumerate(groups):
        total = recv3[begin, part].astype(f32)
        for s in range(begin + 1, end):
            total += recv3[s, part].astype(f32)
        out[g] = jnp.transpose(total) + extra[g]


def part_sides(face_size, both, out_res, out_schur):
    out_res[...] = both[:, :face_size]
    out_schur[...] = both[:, HALF : HALF + face_size]


def on_device(
    interior_res,
    face_res,
    trace_vals,
    stabil,
    element_faces,
    orient,
    lift_matrix,
    face_matrix,
    factors,
):
    sections = lax.axis_size("section")
    columns = lax.axis_size("elem")
    elems, inner = interior_res.shape[3:]
    face_size = face_res.shape[5]
    fnodes = face_matrix.shape[0]
    modes = lift_matrix.shape[1]
    nvar = face_size // fnodes
    chunk = 32
    col_elems = sections * elems
    face_dev = 2 * elems
    col_faces = sections * face_dev
    f32, bf16 = jnp.float32, jnp.bfloat16
    consts, place, classes = structure(modes, fnodes, nvar, chunk)

    dims = (sections, columns, elems, inner, face_size, nvar, chunk)
    out = jax.ShapeDtypeStruct((3, face_size, face_dev), f32)
    vmem = pl.BlockSpec(memory_space=pltpu.VMEM)
    both = pl.pallas_call(
        functools.partial(kernel, dims, place, classes),
        out_shape=jax.ShapeDtypeStruct((3, LANE, face_dev), f32),
        in_specs=[vmem] * 8 + [pl.BlockSpec(memory_space=pl.ANY)] * 2,
        out_specs=vmem,
        scratch_shapes=[
            pltpu.VMEM(factors.shape[2:], bf16),
            pltpu.VMEM(consts.shape, bf16),
            pltpu.VMEM((3, elems, 4, face_size), f32),
            pltpu.VMEM((3, 5, elems, LANE), f32),
            pltpu.VMEM((sections, nvar * nvar, 4, elems), f32),
            pltpu.VMEM((fnodes, 4, modes), f32),
            pltpu.VMEM((sections, 5, elems, LANE), bf16),
            pltpu.VMEM((sections, 5, elems, LANE), bf16),
            pltpu.VMEM((4, 2 * LANE, nvar * LANE), bf16),
            pltpu.VMEM((4, col_elems, (nvar + 1) * LANE), f32),
            pltpu.VMEM((4, col_faces, col_elems), bf16),
            pltpu.VMEM((4, columns * 8, col_elems), f32),
            pltpu.VMEM((columns * 8, LANE), f32),
            pltpu.VMEM((4, col_elems, LANE), f32),
            pltpu.VMEM((col_elems, 2 * LANE), f32),
            pltpu.VMEM((columns, 8, LANE), f32),
            pltpu.VMEM((sections, columns, 8, LANE), f32),
            pltpu.VMEM((sections, 2, face_dev, LANE), bf16),
            pltpu.VMEM((sections, 2, face_dev, LANE), bf16),
            pltpu.SemaphoreType.DMA,
            pltpu.SemaphoreType.DMA,
            pltpu.SemaphoreType.DMA((sections,)),
            pltpu.SemaphoreType.DMA((sections,)),
            pltpu.SemaphoreType.DMA((sections * columns,)),
            pltpu.SemaphoreType.DMA((sections * columns,)),
            pltpu.SemaphoreType.DMA((sections,)),
            pltpu.SemaphoreType.DMA((sections,)),
        ],
        compiler_params=pltpu.CompilerParams(
            collective_id=0, has_side_effects=True, vmem_limit_bytes=56 * 2**20
        ),
    )(
        interior_res[:, 0, 0],
        face_res[:, 0, 0],
        trace_vals[:, 0, 0],
        stabil[0].transpose(0, 3, 2, 1),
        element_faces[0].transpose(0, 2, 1),
        orient[0].transpose(0, 3, 2, 1),
        lift_matrix.transpose(2, 0, 1),
        face_matrix,
        jnp.asarray(consts, bf16),
        factors,
    )
    residual, schur = pl.pallas_call(
        functools.partial(part_sides, face_size),
        out_shape=(out, out),
        in_specs=[vmem],
        out_specs=(vmem, vmem),
    )(both)
    return residual.transpose(0, 2, 1), schur.transpose(0, 2, 1)


def solution(mesh):
    return jax.shard_map(
        on_device,
        mesh=mesh,
        in_specs=(
            P(None, "elem", "section", None, None),
            P(None, "elem", "section", None, None, None),
            P(None, "elem", "section", None, None, None),
            P("elem", None, None, None, None),
            P("elem", None, None, None),
            P("elem", None, None, None, None),
            P(),
            P(),
            P("section", "elem", None, None),
        ),
        out_specs=(P(None, ("section", "elem"), None), P(None, ("section", "elem"), None)),
        check_vma=False,
    )
```
